256 devices in a mesh: pool: 8 (over z), tp: 16 (over y_lo, x, core), rep: 2 (over y_hi).
Axes of the slice: x: 4, y: 4 (y_hi: 2, y_lo: 2; y = y_hi * 2 + y_lo), z: 8, core: 2. Of those that a mesh axis runs over, the one named last changes fastest.
Arguments:
- queries: bfloat16 [2, 8, 4, 256, 16384], P('rep', 'pool', None, None, 'tp'), may hold values from -48 to 48
- pool_cache: bfloat16 [512, 8, 128, 256], P('pool', None, 'tp'), may hold values from -6 to 6
- new_kv: bfloat16 [2, 8, 4, 2, 8, 128, 256], P('rep', 'pool', None, None, None, 'tp'), may hold values from -16 to 16
- block_ids: int32 [2, 8, 4, 12], P('rep'), may hold values from 0 to 511, as said below
- prefix_count: int32 [2, 8], P('rep'), may hold values from 6 to 12, as said below
- new_ids: int32 [2, 8, 4, 2], P('rep'), may hold values from 0 to 63, as said below
Outputs:
- attn_out: bfloat16 [2, 8, 4, 256, 16384], P('rep', 'pool', None, None, 'tp')
- stored_new: bfloat16 [2, 64, 8, 128, 256], P('rep', 'pool', None, 'tp')
The draws below stay inside these ranges and needn't reach their ends.
Inputs may be any that keep to these rules, and one draw needn't show every extreme that they name: `block_ids`: an id names slot id % 64 of holder id // 64. In every list of 12 entries at most 2 entries name one holder, and some holder is named by exactly 2. `prefix_count`: some prompt has all 12 entries live. `new_ids`: within one index of the first dimension every id appears exactly once. The ids of one prompt name each holder id // 8 exactly once.
All inputs are finite; a program needn't handle non-finite values.
Results may differ from the reference program's by a relative error of at most 0.0034.
Values may be sent and summed in bfloat16 or wider, within the bound.
A program may use at most 128 MiB of HBM per device.

```python
import math
import jax
import jax.numpy as jnp
from jax import lax

NH = 128
KVH = 8
HD = 128
BT = 128
LAYERS = 4
NEWB = 2
CAP = 2
SLOTS = 64
N_POOL = 8
N_REP = 2


def draw_queries(key, part):
    key = jax.random.fold_in(key, 11)
    shape = (N_REP, N_POOL, LAYERS, NEWB * BT, NH * HD)
    values = 2.0 * jax.random.truncated_normal(key, -6.0, 6.0, shape, jnp.float32)
    return values.astype(jnp.bfloat16)


def draw_new_kv(key, part):
    key = jax.random.fold_in(key, 12)
    shape = (N_REP, N_POOL, LAYERS, NEWB, KVH, BT, 2 * HD)
    values = jax.random.truncated_normal(key, -4.0, 4.0, shape, jnp.float32)
    return values.astype(jnp.bfloat16)


def draw_block_ids(key, part):
    key = jax.random.fold_in(key, 21)
    list_count = N_REP * N_POOL * LAYERS
    length = 3 * N_POOL // 2
    base_key, hot_key, order_key, place_key, slot_key = jax.random.split(key, 5)
    hot_base = jax.random.randint(base_key, (), 0, N_POOL)
    hot_holder = (hot_base + jax.random.randint(hot_key, (list_count,), 0, max(N_POOL // 4, 1))) % N_POOL
    offsets = jnp.arange((N_POOL - 1) * CAP) // CAP + 1
    shuffled = jax.vmap(lambda single: jax.random.permutation(single, offsets))(jax.random.split(order_key, list_count))
    others = (hot_holder[:, None] + shuffled[:, :length - CAP]) % N_POOL
    sequence = jnp.concatenate([jnp.broadcast_to(hot_holder[:, None], (list_count, CAP)), others], axis=1)
    placing = jax.vmap(lambda single: jax.random.permutation(single, length))(jax.random.split(place_key, list_count))
    sequence = jnp.take_along_axis(sequence, placing, axis=1)
    slot_index = jax.random.randint(slot_key, (list_count, length), 0, SLOTS)
    return (sequence * SLOTS + slot_index).astype(jnp.int32).reshape(N_REP, N_POOL, LAYERS, length)


def draw_prefix_count(key, part):
    key = jax.random.fold_in(key, 22)
    length = 3 * N_POOL // 2
    count_key, index_key = jax.random.split(key)
    counts = jax.random.randint(count_key, (N_REP * N_POOL,), length // 2, length + 1)
    chosen = jax.random.randint(index_key, (), 0, N_REP * N_POOL)
    counts = counts.at[chosen].set(length)
    return counts.astype(jnp.int32).reshape(N_REP, N_POOL)


def draw_new_ids(key, part):
    key = jax.random.fold_in(key, 23)
    entries = LAYERS * NEWB
    per_holder = entries // N_POOL
    slot_key, order_key = jax.random.split(key)
    slot_perm = jax.vmap(lambda single: jax.random.permutation(single, entries))(jax.random.split(slot_key, N_REP * N_POOL))
    slot_perm = slot_perm.reshape(N_REP, N_POOL, N_POOL, per_holder).transpose(0, 2, 1, 3)
    holder_base = (jnp.arange(N_POOL) * entries)[None, None, :, None]
    listed = (slot_perm + holder_base).reshape(N_REP * N_POOL, entries)
    placing = jax.vmap(lambda single: jax.random.permutation(single, entries))(jax.random.split(order_key, N_REP * N_POOL))
    listed = jnp.take_along_axis(listed, placing, axis=1)
    return listed.astype(jnp.int32).reshape(N_REP, N_POOL, LAYERS, NEWB)


def levels(key, shape, cuts, least, top_value):
    def one(position, blocks):
        heights = jax.random.uniform(jax.random.fold_in(jax.random.fold_in(key, 6), position), (blocks,), jnp.float32, least / len(cuts), top_value / len(cuts))
        return jnp.repeat(jnp.exp(heights), shape[position] // blocks).reshape((-1,) + (1,) * (len(shape) - position - 1))

    gain = one(*cuts[0])
    for cut in cuts[1:]:
        gain = gain * one(*cut)
    return gain


def gaussian(own_key, extent, spread, bound, pieces=(), dtype=jnp.bfloat16):
    values = jax.random.normal(own_key, extent, jnp.float32) * spread
    if len(pieces) > 0:
        values = levels(own_key, extent, pieces, -0.22, 0.18) * values
    return jnp.clip(values, min=-bound, max=bound).astype(dtype)


def setup_inputs(seed: int = 0) -> dict:
    key_of = jax.random.split(jax.random.key(seed), 7)
    queries = draw_queries(jax.random.fold_in(key_of[6], 71), 0)
    pool_cache = gaussian(key_of[1], (N_POOL * SLOTS, KVH, BT, 2 * HD), 1.0, 6.0, ((0, 8), (2, 16)))
    new_kv = draw_new_kv(jax.random.fold_in(key_of[6], 71), 0)
    block_ids = draw_block_ids(jax.random.fold_in(key_of[6], 71), 0)
    prefix_count = draw_prefix_count(jax.random.fold_in(key_of[6], 71), 0)
    new_ids = draw_new_ids(jax.random.fold_in(key_of[6], 71), 0)
    return {"queries": queries, "pool_cache": pool_cache, "new_kv": new_kv, "block_ids": block_ids, "prefix_count": prefix_count, "new_ids": new_ids}


def head_attend(query_rows, key_value, visible, scale):
    head_dim = query_rows.shape[-1]
    key_part = key_value[:, :head_dim].astype(jnp.float32)
    value_part = key_value[:, head_dim:].astype(jnp.float32)
    scores = jnp.einsum('iqd,nd->iqn', query_rows.astype(jnp.float32), key_part) * scale
    scores = jnp.where(visible[:, None, :], scores, -1e+30)
    highest = lax.optimization_barrier(jnp.max(scores, axis=-1, keepdims=True))
    weights = jnp.exp(scores - highest)
    totals = lax.optimization_barrier(jnp.sum(weights, axis=-1))
    rounded = lax.optimization_barrier(weights.astype(jnp.bfloat16)).astype(jnp.float32)
    mixed = jnp.einsum('iqn,nd->iqd', rounded, value_part) / totals[..., None]
    return mixed.astype(jnp.bfloat16)

def reference(queries, pool_cache, new_kv, block_ids, prefix_count, new_ids):
    n_rep, n_pool, layers, span, width = queries.shape
    kv_heads = pool_cache.shape[1]
    block = pool_cache.shape[2]
    width2 = pool_cache.shape[3]
    head_dim = width2 // 2
    head_count = width // head_dim
    group_size = head_count // kv_heads
    list_length = block_ids.shape[3]
    new_blocks = new_kv.shape[3]
    scale = 1.0 / math.sqrt(head_dim)
    list_count = n_rep * n_pool * layers
    flat_queries = queries.reshape(list_count, span, kv_heads, group_size, head_dim).transpose(0, 2, 1, 3, 4)
    flat_new = new_kv.reshape(list_count, new_blocks, kv_heads, block, width2)
    flat_ids = block_ids.reshape(list_count, list_length)
    flat_counts = jnp.repeat(prefix_count.reshape(-1), layers)
    causal = jnp.arange(span)[None, :] <= jnp.arange(span)[:, None]
    prefix_block = jnp.arange(list_length * block) // block

    def one_list(packed):
        query_heads, fresh_blocks, entries, live_count = packed
        prefix = pool_cache[entries].transpose(1, 0, 2, 3).reshape(kv_heads, list_length * block, width2)
        recent = fresh_blocks.transpose(1, 0, 2, 3).reshape(kv_heads, span, width2)
        key_value = jnp.concatenate([prefix, recent], axis=1)
        prefix_live = jnp.broadcast_to((prefix_block < live_count)[None, :], (span, list_length * block))
        visible = jnp.concatenate([prefix_live, causal], axis=1)

        def one_head(paired):
            return head_attend(paired[0], paired[1], visible, scale)
        mixed = lax.map(one_head, (query_heads, key_value))
        return mixed.transpose(1, 0, 2, 3).reshape(span, width)
    attn_out = lax.map(one_list, (flat_queries, flat_new, flat_ids, flat_counts)).reshape(queries.shape)
    slot_total = n_pool * layers * new_blocks
    targets = new_ids.reshape(n_rep, -1)
    payload = new_kv.reshape(n_rep, -1, kv_heads, block, width2)
    stored_new = jnp.zeros((n_rep, slot_total, kv_heads, block, width2), jnp.bfloat16)
    stored_new = stored_new.at[jnp.arange(n_rep)[:, None], targets].set(payload)
    return (attn_out, stored_new)
```

```python
import functools
import math

import jax
import jax.numpy as jnp
from jax import lax
from jax.experimental import pallas as pl
from jax.experimental.pallas import tpu as pltpu
from jax.sharding import PartitionSpec as P

MESH = pl.DeviceIdType.MESH
POOL = 8
CHIPS = 8
CORES = 2
LAYERS = 4
LIST = 12
SLOTS = 64
TOK = 8
CAP = 2
ROWS = CAP * TOK
HEADS = 8
HD = 128
QH = 8
SPAN = 256
ENTRIES = 8
DISTANCE = (4, 3, 5, 2, 6, 1, 7)
FIRST_FAR = 2
SOURCES = FIRST_FAR + len(DISTANCE)
GROUPS = ((0, 2), (2, 3), (3, 5), (5, 7), (7, 9))
N_GROUPS = len(GROUPS)
MASKED = -1e30
TO_LOG2 = math.log2(math.e) / math.sqrt(HD)


def interleave(first, second):
    first = first.astype(jnp.float32)
    second = second.astype(jnp.float32)
    pieces = []
    for head in range(HEADS):
        rows = slice(head * TOK, (head + 1) * TOK)
        pieces += [first[rows], second[rows]]
    return jnp.concatenate(pieces, axis=0).astype(jnp.bfloat16)


def kernel(
    ids, counts, new_ids, q_in, cache_in, new_in, attn_out, stored_out,
    cache, new, q, zsend, zbuf, kv, nsend, nrecv, placed, attn, top, total, acc,
    in_sem, zs, zr, ps, pr, ss, sr, ns, nr, out_sem,
):
    pool = lax.axis_index("pool")
    tp = lax.axis_index("tp")
    core = lax.rem(tp, CORES)
    chip = lax.div(tp, CORES)

    def pool_peer(distance):
        return lax.rem(pool + distance, POOL)

    def chip_peer(step):
        return lax.rem(chip + step, CHIPS)

    sibling = {"tp": chip * CORES + 1 - core}

    loads = [
        pltpu.make_async_copy(cache_in, cache, in_sem.at[0]),
        pltpu.make_async_copy(new_in, new, in_sem.at[1]),
        pltpu.make_async_copy(q_in, q, in_sem.at[2]),
    ]
    for load in loads:
        load.start()

    barrier = pltpu.get_barrier_semaphore()
    for distance in DISTANCE:
        pl.semaphore_signal(barrier, inc=1, device_id={"pool": pool_peer(distance)}, device_id_type=MESH)
    for step in range(1, CHIPS):
        pl.semaphore_signal(
            barrier, inc=1, device_id={"tp": chip_peer(step) * CORES + core}, device_id_type=MESH
        )
    pl.semaphore_signal(barrier, inc=1, device_id=sibling, device_id_type=MESH)

    def prepare(layer):
        for place in range(FIRST_FAR - 1, SOURCES):
            distance = 0 if place < FIRST_FAR else DISTANCE[place - FIRST_FAR]
            prompt = pool_peer(distance)
            live = counts[0, prompt]
            first = jnp.int32(0)
            last = jnp.int32(0)
            found = [
                ((ids[prompt, layer, j] >> 6) == pool) & (j < live) for j in range(LIST)
            ]
            slot = [ids[prompt, layer, j] & (SLOTS - 1) for j in range(LIST)]
            for j in range(LIST):
                last = jnp.where(found[j], slot[j], last)
                first = jnp.where(found[LIST - 1 - j], slot[LIST - 1 - j], first)
            rows = interleave(cache[first], cache[last])
            if place < FIRST_FAR:
                zbuf[layer, place] = rows
            else:
                zsend[layer, place - FIRST_FAR] = rows
        zbuf[layer, 0] = interleave(new[2 * layer], new[2 * layer + 1])

    def z_copy(layer, index):
        return pltpu.make_async_remote_copy(
            src_ref=zsend.at[layer, index],
            dst_ref=zbuf.at[layer, FIRST_FAR + index],
            send_sem=zs.at[layer, index],
            recv_sem=zr.at[layer, index],
            device_id={"pool": pool_peer(DISTANCE[index])},
            device_id_type=MESH,
        )

    def n_copy(index):
        return pltpu.make_async_remote_copy(
            src_ref=nsend.at[index],
            dst_ref=nrecv.at[1 + index],
            send_sem=ns.at[index],
            recv_sem=nr.at[index],
            device_id={"pool": pool_peer(DISTANCE[index])},
            device_id_type=MESH,
        )

    def plane_copy(layer, group, step):
        low, high = GROUPS[group]
        target = chip_peer(step)
        return pltpu.make_async_remote_copy(
            src_ref=zbuf.at[layer, pl.ds(low, high - low), pl.ds(pl.multiple_of(target * ROWS, ROWS), ROWS)],
            dst_ref=kv.at[
                layer,
                pl.ds(low, high - low),
                pl.ds(pl.multiple_of((core * CHIPS + chip) * ROWS, ROWS), ROWS),
            ],
            send_sem=ps.at[layer, group, step - 1],
            recv_sem=pr.at[layer, group, step - 1],
            device_id={"tp": target * CORES + core},
            device_id_type=MESH,
        )

    def sibling_copy(layer, group):
        low, high = GROUPS[group]
        half = (
            layer,
            pl.ds(low, high - low),
            pl.ds(pl.multiple_of(core * CHIPS * ROWS, CHIPS * ROWS), CHIPS * ROWS),
        )
        return pltpu.make_async_remote_copy(
            src_ref=kv.at[half],
            dst_ref=kv.at[half],
            send_sem=ss.at[layer, group],
            recv_sem=sr.at[layer, group],
            device_id=sibling,
            device_id_type=MESH,
        )

    def z_send(layer):
        for index in range(len(DISTANCE)):
            z_copy(layer, index).start()

    def spread(layer, group):
        low, high = GROUPS[group]
        for place in range(max(low, FIRST_FAR), high):
            z_copy(layer, place - FIRST_FAR).wait_recv()
        for step in range(1, CHIPS):
            plane_copy(layer, group, step).start()
        mine = zbuf[layer, pl.ds(low, high - low), pl.ds(pl.multiple_of(chip * ROWS, ROWS), ROWS)]
        kv[
            layer,
            pl.ds(low, high - low),
            pl.ds(pl.multiple_of((core * CHIPS + chip) * ROWS, ROWS), ROWS),
        ] = mine

    def share(layer, group):
        for step in range(1, CHIPS):
            plane_copy(layer, group, step).wait_recv()
        sibling_copy(layer, group).start()

    def attend(layer, group):
        low, high = GROUPS[group]
        count = high - low
        keys = CORES * CHIPS * ROWS
        sibling_copy(layer, group).wait_recv()
        lane = lax.broadcasted_iota(jnp.int32, (1, keys), 1)
        slot = (lane >> 3) & 1
        biases = []
        for place in range(low, high):
            if place == 0:
                position = slot * 128 + (((lane >> 4) & 7) * 2 + (lane >> 7)) * TOK + (lane & 7)
                row = lax.broadcasted_iota(jnp.int32, (SPAN, keys), 0)
                biases.append(jnp.where(position <= row, 0.0, MASKED))
                continue
            distance = 0 if place < FIRST_FAR else DISTANCE[place - FIRST_FAR]
            holder = lax.rem(pool + POOL - distance, POOL)
            live = counts[0, pool]
            named = jnp.int32(0)
            for j in range(LIST):
                hit = ((ids[pool, layer, j] >> 6) == holder) & (j < live)
                named += jnp.where(hit, 1, 0)
            biases.append(jnp.where(slot < named, 0.0, MASKED))

        def one_head(head, carry):
            columns = pl.ds(pl.multiple_of(head * HD, HD), HD)
            rows = q[layer, :, columns]
            scores = []
            for index in range(count):
                block = lax.dot_general(
                    rows,
                    kv[layer, low + index, :, :HD],
                    (((1,), (1,)), ((), ())),
                    preferred_element_type=jnp.float32,
                )
                scores.append(block * TO_LOG2 + biases[index])
            highest = jnp.max(functools.reduce(jnp.maximum, scores), axis=1, keepdims=True)
            if group > 0:
                before = top[head]
                highest = jnp.maximum(highest, before[:, :1])
            weights = [jnp.exp2(block - highest) for block in scores]
            added = jnp.sum(functools.reduce(jnp.add, weights), axis=1, keepdims=True)
            mixed = None
            for index in range(count):
                part = jnp.dot(
                    weights[index].astype(jnp.bfloat16),
                    kv[layer, low + index, :, HD:],
                    preferred_element_type=jnp.float32,
                )
                mixed = part if mixed is None else mixed + part
            if group > 0:
                shrink = jnp.exp2(before[:, :1] - highest)
                added = added + shrink * total[head][:, :1]
                mixed = mixed + shrink * acc[head]
            if group < N_GROUPS - 1:
                top[head] = jnp.broadcast_to(highest, (SPAN, HD))
                total[head] = jnp.broadcast_to(added, (SPAN, HD))
                acc[head] = mixed
            else:
                attn[layer, :, columns] = (mixed / added).astype(jnp.bfloat16)
            return carry

        lax.fori_loop(0, QH, one_head, 0)

    def attn_copy(layer):
        return pltpu.make_async_copy(attn.at[layer], attn_out.at[layer], out_sem.at[layer])

    loads[0].wait()
    loads[1].wait()
    prepare(0)
    pl.semaphore_wait(barrier, len(DISTANCE) + CHIPS)
    z_send(0)

    @pl.loop(1, LAYERS)
    def _(layer):
        prepare(layer)
        z_send(layer)

    for place in range(POOL):
        distance = 0 if place == 0 else DISTANCE[place - 1]
        holder = pool_peer(distance)
        entry = jnp.int32(0)
        for e in range(ENTRIES):
            entry = jnp.where((new_ids[pool, e // 2, e % 2] >> 3) == holder, e, entry)
        if place == 0:
            nrecv[0] = new[entry]
        else:
            nsend[place - 1] = new[entry]
            n_copy(place - 1).start()
    origin = [jnp.int32(0)] * ENTRIES
    for place in range(POOL):
        distance = 0 if place == 0 else DISTANCE[place - 1]
        prompt = lax.rem(pool + POOL - distance, POOL)
        slot = jnp.int32(0)
        for e in range(ENTRIES):
            written = new_ids[prompt, e // 2, e % 2]
            slot = jnp.where((written >> 3) == pool, written & 7, slot)
        origin = [jnp.where(slot == j, place, origin[j]) for j in range(ENTRIES)]

    spread(0, 0)
    spread(0, 1)
    share(0, 0)
    loads[2].wait()

    @pl.loop(0, LAYERS)
    def _(layer):
        for group in range(N_GROUPS):
            if group + 2 < N_GROUPS:
                spread(layer, group + 2)
            else:

                @pl.when(layer < LAYERS - 1)
                def _():
                    spread(layer + 1, group + 2 - N_GROUPS)

            if group + 1 < N_GROUPS:
                share(layer, group + 1)
            else:

                @pl.when(layer < LAYERS - 1)
                def _():
                    share(layer + 1, 0)

            attend(layer, group)
        attn_copy(layer).start()

    for index in range(len(DISTANCE)):
        n_copy(index).wait_recv()
    for j in range(ENTRIES):
        placed[j] = nrecv[origin[j]]
    stored_copy = pltpu.make_async_copy(placed, stored_out, out_sem.at[LAYERS])
    stored_copy.start()

    @pl.loop(0, LAYERS)
    def _(layer):
        for index in range(len(DISTANCE)):
            z_copy(layer, index).wait_send()
        for group in range(N_GROUPS):
            for step in range(1, CHIPS):
                plane_copy(layer, group, step).wait_send()
            sibling_copy(layer, group).wait_send()
        attn_copy(layer).wait()

    for index in range(len(DISTANCE)):
        n_copy(index).wait_send()
    stored_copy.wait()


def body(queries, pool_cache, new_kv, block_ids, prefix_count, new_ids):
    smem = pl.BlockSpec(memory_space=pltpu.SMEM)
    hbm = pl.BlockSpec(memory_space=pl.ANY)
    bf16 = jnp.bfloat16
    far = len(DISTANCE)
    attn, stored = pl.pallas_call(
        kernel,
        out_shape=(
            jax.ShapeDtypeStruct((LAYERS, SPAN, QH * HD), bf16),
            jax.ShapeDtypeStruct((ENTRIES, HEADS * TOK, 2 * HD), bf16),
        ),
        in_specs=[smem, smem, smem, hbm, hbm, hbm],
        out_specs=(hbm, hbm),
        scratch_shapes=[
            pltpu.VMEM((SLOTS, HEADS * TOK, 2 * HD), bf16),
            pltpu.VMEM((ENTRIES, HEADS * TOK, 2 * HD), bf16),
            pltpu.VMEM((LAYERS, SPAN, QH * HD), bf16),
            pltpu.VMEM((LAYERS, far, HEADS * ROWS, 2 * HD), bf16),
            pltpu.VMEM((LAYERS, SOURCES, HEADS * ROWS, 2 * HD), bf16),
            pltpu.VMEM((LAYERS, SOURCES, CORES * CHIPS * ROWS, 2 * HD), bf16),
            pltpu.VMEM((far, HEADS * TOK, 2 * HD), bf16),
            pltpu.VMEM((POOL, HEADS * TOK, 2 * HD), bf16),
            pltpu.VMEM((ENTRIES, HEADS * TOK, 2 * HD), bf16),
            pltpu.VMEM((LAYERS, SPAN, QH * HD), bf16),
            pltpu.VMEM((QH, SPAN, HD), jnp.float32),
            pltpu.VMEM((QH, SPAN, HD), jnp.float32),
            pltpu.VMEM((QH, SPAN, HD), jnp.float32),
            pltpu.SemaphoreType.DMA((3,)),
            pltpu.SemaphoreType.DMA((LAYERS, far)),
            pltpu.SemaphoreType.DMA((LAYERS, far)),
            pltpu.SemaphoreType.DMA((LAYERS, N_GROUPS, CHIPS - 1)),
            pltpu.SemaphoreType.DMA((LAYERS, N_GROUPS, CHIPS - 1)),
            pltpu.SemaphoreType.DMA((LAYERS, N_GROUPS)),
            pltpu.SemaphoreType.DMA((LAYERS, N_GROUPS)),
            pltpu.SemaphoreType.DMA((far,)),
            pltpu.SemaphoreType.DMA((far,)),
            pltpu.SemaphoreType.DMA((LAYERS + 1,)),
        ],
        compiler_params=pltpu.CompilerParams(
            collective_id=0, has_side_effects=True, vmem_limit_bytes=48 << 20
        ),
    )(
        block_ids[0],
        prefix_count,
        new_ids[0],
        queries[0, 0],
        pool_cache.reshape(SLOTS, HEADS * TOK, 2 * HD),
        new_kv.reshape(ENTRIES, HEADS * TOK, 2 * HD),
    )
    return attn[None, None], stored.reshape(1, ENTRIES, HEADS, TOK, 2 * HD)


def solution(mesh):
    in_specs = (
        P("rep", "pool", None, None, "tp"),
        P("pool", None, "tp", None),
        P("rep", "pool", None, None, None, "tp", None),
        P("rep", None, None, None),
        P("rep", None),
        P("rep", None, None, None),
    )
    out_specs = (P("rep", "pool", None, None, "tp"), P("rep", "pool", None, "tp", None))
    return jax.shard_map(body, mesh=mesh, in_specs=in_specs, out_specs=out_specs, check_vma=False)
```

```python
import functools
import math

import jax
import jax.numpy as jnp
from jax import lax
from jax.experimental import pallas as pl
from jax.experimental.pallas import tpu as pltpu
from jax.sharding import PartitionSpec as P

MESH = pl.DeviceIdType.MESH
POOL = 8
CHIPS = 8
CORES = 2
LAYERS = 4
LIST = 12
SLOTS = 64
TOK = 8
CAP = 2
ROWS = CAP * TOK
HEADS = 8
HD = 128
QH = 8
SPAN = 256
ENTRIES = 8
DISTANCE = (4, 3, 5, 2, 6, 1, 7)
FIRST_FAR = 2
SOURCES = FIRST_FAR + len(DISTANCE)
GROUPS = ((0, 2), (2, 3), (3, 5), (5, 7), (7, 9))
N_GROUPS = len(GROUPS)
KEYS = CORES * CHIPS * ROWS
MASKED = -1e30
TO_LOG2 = math.log2(math.e) / math.sqrt(HD)


def interleave(first, second):
    first = first.astype(jnp.float32)
    second = second.astype(jnp.float32)
    pieces = []
    for head in range(HEADS):
        rows = slice(head * TOK, (head + 1) * TOK)
        pieces += [first[rows], second[rows]]
    return jnp.concatenate(pieces, axis=0).astype(jnp.bfloat16)


def kernel(
    ids_in, counts_in, new_ids_in, q_in, cache_in, new_in, attn_out, stored_out,
    ids, counts, new_ids,
    cache, new, q, zsend, zbuf, kv, nsend, nrecv, placed, attn, top, total, acc, qt, flipped, causal,
    in_sem, zs, zr, ps, pr, ss, sr, ns, nr, out_sem,
):
    pool = lax.axis_index("pool")
    tp = lax.axis_index("tp")
    core = lax.rem(tp, CORES)
    chip = lax.div(tp, CORES)

    def pool_peer(distance):
        return lax.rem(pool + distance, POOL)

    def chip_peer(step):
        return lax.rem(chip + step, CHIPS)

    sibling = {"tp": chip * CORES + 1 - core}

    moves = ((ids_in, ids), (counts_in, counts), (new_ids_in, new_ids), (cache_in, cache), (new_in, new), (q_in, q))
    loads = [pltpu.make_async_copy(*move, in_sem.at[index]) for index, move in enumerate(moves)]
    for load in loads:
        load.start()

    barrier = pltpu.get_barrier_semaphore()
    for distance in DISTANCE:
        pl.semaphore_signal(barrier, inc=1, device_id={"pool": pool_peer(distance)}, device_id_type=MESH)
    for step in range(1, CHIPS):
        pl.semaphore_signal(
            barrier, inc=1, device_id={"tp": chip_peer(step) * CORES + core}, device_id_type=MESH
        )
    pl.semaphore_signal(barrier, inc=1, device_id=sibling, device_id_type=MESH)

    def prepare(layer):
        for place in range(FIRST_FAR - 1, SOURCES):
            distance = 0 if place < FIRST_FAR else DISTANCE[place - FIRST_FAR]
            prompt = pool_peer(distance)
            live = counts[0, prompt]
            first = jnp.int32(0)
            last = jnp.int32(0)
            found = [
                ((ids[prompt, layer, j] >> 6) == pool) & (j < live) for j in range(LIST)
            ]
            slot = [ids[prompt, layer, j] & (SLOTS - 1) for j in range(LIST)]
            for j in range(LIST):
                last = jnp.where(found[j], slot[j], last)
                first = jnp.where(found[LIST - 1 - j], slot[LIST - 1 - j], first)
            rows = interleave(cache[first], cache[last])
            if place < FIRST_FAR:
                zbuf[layer, place] = rows
            else:
                zsend[layer, place - FIRST_FAR] = rows
        zbuf[layer, 0] = interleave(new[2 * layer], new[2 * layer + 1])

    def z_copy(layer, index):
        return pltpu.make_async_remote_copy(
            src_ref=zsend.at[layer, index],
            dst_ref=zbuf.at[layer, FIRST_FAR + index],
            send_sem=zs.at[layer],
            recv_sem=zr.at[layer, index],
            device_id={"pool": pool_peer(DISTANCE[index])},
            device_id_type=MESH,
        )

    def n_copy(index):
        return pltpu.make_async_remote_copy(
            src_ref=nsend.at[index],
            dst_ref=nrecv.at[1 + index],
            send_sem=ns.at[0],
            recv_sem=nr.at[0],
            device_id={"pool": pool_peer(DISTANCE[index])},
            device_id_type=MESH,
        )

    def whole(part, send_sem, recv_sem):
        return pltpu.make_async_remote_copy(
            src_ref=part,
            dst_ref=part,
            send_sem=send_sem,
            recv_sem=recv_sem,
            device_id=sibling,
            device_id_type=MESH,
        )

    def plane_copy(layer, group, step):
        low, high = GROUPS[group]
        target = chip_peer(step)
        return pltpu.make_async_remote_copy(
            src_ref=zbuf.at[layer, pl.ds(low, high - low), pl.ds(pl.multiple_of(target * ROWS, ROWS), ROWS)],
            dst_ref=kv.at[
                layer,
                pl.ds(low, high - low),
                pl.ds(pl.multiple_of((core * CHIPS + chip) * ROWS, ROWS), ROWS),
            ],
            send_sem=ps.at[layer, group],
            recv_sem=pr.at[layer, group],
            device_id={"tp": target * CORES + core},
            device_id_type=MESH,
        )

    def plane_copies(layer, group):
        low, high = GROUPS[group]
        part = zbuf.at[layer, pl.ds(low, high - low), pl.ds(0, (CHIPS - 1) * ROWS)]
        return whole(part, ps.at[layer, group], pr.at[layer, group])

    def sibling_copy(layer, group):
        low, high = GROUPS[group]
        half = (
            layer,
            pl.ds(low, high - low),
            pl.ds(pl.multiple_of(core * CHIPS * ROWS, CHIPS * ROWS), CHIPS * ROWS),
        )
        return pltpu.make_async_remote_copy(
            src_ref=kv.at[half],
            dst_ref=kv.at[half],
            send_sem=ss.at[layer, group],
            recv_sem=sr.at[layer, group],
            device_id=sibling,
            device_id_type=MESH,
        )

    def z_send(layer):
        for index in range(len(DISTANCE)):
            z_copy(layer, index).start()

    def spread(layer, group):
        low, high = GROUPS[group]
        for place in range(max(low, FIRST_FAR), high):
            z_copy(layer, place - FIRST_FAR).wait_recv()
        for step in range(1, CHIPS):
            plane_copy(layer, group, step).start()
        mine = zbuf[layer, pl.ds(low, high - low), pl.ds(pl.multiple_of(chip * ROWS, ROWS), ROWS)]
        kv[
            layer,
            pl.ds(low, high - low),
            pl.ds(pl.multiple_of((core * CHIPS + chip) * ROWS, ROWS), ROWS),
        ] = mine

    def share(layer, group):
        plane_copies(layer, group).wait_recv()
        sibling_copy(layer, group).start()

    def attend(layer, group):
        low, high = GROUPS[group]
        count = high - low
        sibling_copy(layer, group).wait_recv()
        biases = []
        for place in range(low, high):
            if place == 0:
                biases.append(None)
                continue
            distance = 0 if place < FIRST_FAR else DISTANCE[place - FIRST_FAR]
            holder = lax.rem(pool + POOL - distance, POOL)
            live = counts[0, pool]
            named = jnp.int32(0)
            for j in range(LIST):
                hit = ((ids[pool, layer, j] >> 6) == holder) & (j < live)
                named += jnp.where(hit, 1, 0)
            biases.append([jnp.where(slot < named, 0.0, MASKED) for slot in range(CAP)])
        for index in range(count):
            values = kv[layer, low + index, :, HD:].astype(jnp.float32)
            flipped[:, index * KEYS : (index + 1) * KEYS] = values.T.astype(jnp.bfloat16)

        def score(head):
            rows = qt[layer, head]
            scores = []
            for index in range(count):
                block = jnp.dot(
                    kv[layer, low + index, :, :HD], rows, preferred_element_type=jnp.float32
                )
                if biases[index] is None:
                    block = block + causal[...]
                scores.append(block.reshape(KEYS // ROWS, CAP, TOK, SPAN))
            return scores

        def weigh(head, scores):
            highest = None
            for block, bias in zip(scores, biases):
                peak = jnp.max(block, axis=0)
                if bias is None:
                    peak = jnp.maximum(peak[0], peak[1])
                else:
                    peak = jnp.maximum(peak[0] + bias[0], peak[1] + bias[1])
                highest = peak if highest is None else jnp.maximum(highest, peak)
            highest = jnp.max(highest, axis=0, keepdims=True) * TO_LOG2
            shrink = None
            if group > 0:
                before = top[head]
                highest = jnp.maximum(highest, before)
                shrink = jnp.exp2(before - highest)
            weights = []
            added = None
            for block, bias in zip(scores, biases):
                shifts = [highest] * CAP if bias is None else [highest - x for x in bias]
                shift = jnp.stack([jnp.broadcast_to(x, (TOK, SPAN)) for x in shifts])
                weight = jnp.exp2(block * TO_LOG2 - shift[None])
                part = jnp.sum(weight, axis=(0, 1))
                added = part if added is None else added + part
                weights.append(weight.reshape(KEYS, SPAN).astype(jnp.bfloat16))
            weights = jnp.concatenate(weights, axis=0) if count > 1 else weights[0]
            added = jnp.sum(added, axis=0, keepdims=True)
            if group > 0:
                added = added + shrink * total[head]
            total[head] = added
            top[head] = highest
            return weights, shrink

        def mix(head, weights, shrink):
            mixed = jnp.dot(
                flipped[:, : count * KEYS], weights, preferred_element_type=jnp.float32
            )
            if group > 0:
                mixed = mixed + shrink * acc[head]
            if group < N_GROUPS - 1:
                acc[head] = mixed
            else:
                attn[layer, :, head * HD : (head + 1) * HD] = (mixed / total[head]).T.astype(jnp.bfloat16)

        scores = [score(head) for head in range(QH)]
        weights = [weigh(head, scores[head]) for head in range(QH)]
        for head in range(QH):
            mix(head, *weights[head])

    def attn_copy(layer):
        return pltpu.make_async_copy(attn.at[layer], attn_out.at[layer], out_sem.at[layer])

    for load in loads[:5]:
        load.wait()
    prepare(0)
    pl.semaphore_wait(barrier, len(DISTANCE) + CHIPS)
    z_send(0)

    @pl.loop(1, LAYERS)
    def _(layer):
        prepare(layer)
        z_send(layer)

    for place in range(POOL):
        distance = 0 if place == 0 else DISTANCE[place - 1]
        holder = pool_peer(distance)
        entry = jnp.int32(0)
        for e in range(ENTRIES):
            entry = jnp.where((new_ids[e // 2, e % 2, pool] >> 3) == holder, e, entry)
        if place == 0:
            nrecv[0] = new[entry]
        else:
            nsend[place - 1] = new[entry]
            n_copy(place - 1).start()
    origin = [jnp.int32(0)] * ENTRIES
    for place in range(POOL):
        distance = 0 if place == 0 else DISTANCE[place - 1]
        prompt = lax.rem(pool + POOL - distance, POOL)
        slot = jnp.int32(0)
        for e in range(ENTRIES):
            written = new_ids[e // 2, e % 2, prompt]
            slot = jnp.where((written >> 3) == pool, written & 7, slot)
        origin = [jnp.where(slot == j, place, origin[j]) for j in range(ENTRIES)]

    spread(0, 0)

    row = lax.broadcasted_iota(jnp.int32, (KEYS, SPAN), 0)
    position = ((row >> 3) & 1) * 128 + (((row >> 4) & 7) * 2 + (row >> 7)) * TOK + (row & 7)
    query = lax.broadcasted_iota(jnp.int32, (KEYS, SPAN), 1)
    causal[...] = jnp.where(position <= query, 0.0, MASKED)
    loads[5].wait()

    @pl.loop(0, LAYERS)
    def _(layer):
        @pl.loop(0, QH)
        def _(head):
            columns = pl.ds(pl.multiple_of(head * HD, HD), HD)
            qt[layer, head] = q[layer, :, columns].astype(jnp.float32).T.astype(jnp.bfloat16)

    spread(0, 1)
    share(0, 0)

    @pl.loop(0, LAYERS)
    def _(layer):
        for group in range(N_GROUPS):
            if group + 2 < N_GROUPS:
                spread(layer, group + 2)
            else:

                @pl.when(layer < LAYERS - 1)
                def _():
                    spread(layer + 1, group + 2 - N_GROUPS)

            if group + 1 < N_GROUPS:
                share(layer, group + 1)
            else:

                @pl.when(layer < LAYERS - 1)
                def _():
                    share(layer + 1, 0)

            attend(layer, group)
        attn_copy(layer).start()

    whole(nsend, ns.at[0], nr.at[0]).wait_recv()
    for j in range(ENTRIES):
        placed[j] = nrecv[origin[j]]
    stored_copy = pltpu.make_async_copy(placed, stored_out, out_sem.at[LAYERS])
    stored_copy.start()

    @pl.loop(0, LAYERS)
    def _(layer):
        whole(zsend.at[layer], zs.at[layer], zr.at[layer, 0]).wait_send()
        for group in range(N_GROUPS):
            plane_copies(layer, group).wait_send()
            sibling_copy(layer, group).wait_send()
        attn_copy(layer).wait()

    whole(nsend, ns.at[0], nr.at[0]).wait_send()
    stored_copy.wait()


def body(queries, pool_cache, new_kv, block_ids, prefix_count, new_ids):
    hbm = pl.BlockSpec(memory_space=pltpu.HBM)
    anywhere = pl.BlockSpec(memory_space=pl.ANY)
    bf16 = jnp.bfloat16
    far = len(DISTANCE)
    attn, stored = pl.pallas_call(
        kernel,
        out_shape=(
            jax.ShapeDtypeStruct((LAYERS, SPAN, QH * HD), bf16),
            jax.ShapeDtypeStruct((ENTRIES, HEADS * TOK, 2 * HD), bf16),
        ),
        in_specs=[hbm] * 6,
        out_specs=(anywhere, anywhere),
        scratch_shapes=[
            pltpu.SMEM((POOL, LAYERS, LIST), jnp.int32),
            pltpu.SMEM((1, POOL), jnp.int32),
            pltpu.SMEM((LAYERS, ENTRIES // LAYERS, POOL), jnp.int32),
            pltpu.VMEM((SLOTS, HEADS * TOK, 2 * HD), bf16),
            pltpu.VMEM((ENTRIES, HEADS * TOK, 2 * HD), bf16),
            pltpu.VMEM((LAYERS, SPAN, QH * HD), bf16),
            pltpu.VMEM((LAYERS, far, HEADS * ROWS, 2 * HD), bf16),
            pltpu.VMEM((LAYERS, SOURCES, HEADS * ROWS, 2 * HD), bf16),
            pltpu.VMEM((LAYERS, SOURCES, CORES * CHIPS * ROWS, 2 * HD), bf16),
            pltpu.VMEM((far, HEADS * TOK, 2 * HD), bf16),
            pltpu.VMEM((POOL, HEADS * TOK, 2 * HD), bf16),
            pltpu.VMEM((ENTRIES, HEADS * TOK, 2 * HD), bf16),
            pltpu.VMEM((LAYERS, SPAN, QH * HD), bf16),
            pltpu.VMEM((QH, 1, SPAN), jnp.float32),
            pltpu.VMEM((QH, 1, SPAN), jnp.float32),
            pltpu.VMEM((QH, HD, SPAN), jnp.float32),
            pltpu.VMEM((LAYERS, QH, HD, SPAN), bf16),
            pltpu.VMEM((HD, 2 * KEYS), bf16),
            pltpu.VMEM((KEYS, SPAN), jnp.float32),
            pltpu.SemaphoreType.DMA((6,)),
            pltpu.SemaphoreType.DMA((LAYERS,)),
            pltpu.SemaphoreType.DMA((LAYERS, far)),
            pltpu.SemaphoreType.DMA((LAYERS, N_GROUPS)),
            pltpu.SemaphoreType.DMA((LAYERS, N_GROUPS)),
            pltpu.SemaphoreType.DMA((LAYERS, N_GROUPS)),
            pltpu.SemaphoreType.DMA((LAYERS, N_GROUPS)),
            pltpu.SemaphoreType.DMA((1,)),
            pltpu.SemaphoreType.DMA((1,)),
            pltpu.SemaphoreType.DMA((LAYERS + 1,)),
        ],
        compiler_params=pltpu.CompilerParams(
            collective_id=0, has_side_effects=True, vmem_limit_bytes=60 << 20
        ),
    )(
        block_ids[0],
        prefix_count,
        new_ids[0].transpose(1, 2, 0),
        queries[0, 0],
        pool_cache.reshape(SLOTS, HEADS * TOK, 2 * HD),
        new_kv.reshape(ENTRIES, HEADS * TOK, 2 * HD),
    )
    return attn[None, None], stored.reshape(1, ENTRIES, HEADS, TOK, 2 * HD)


def solution(mesh):
    in_specs = (
        P("rep", "pool", None, None, "tp"),
        P("pool", None, "tp", None),
        P("rep", "pool", None, None, None, "tp", None),
        P("rep", None, None, None),
        P("rep", None),
        P("rep", None, None, None),
    )
    out_specs = (P("rep", "pool", None, None, "tp"), P("rep", "pool", None, "tp", None))
    return jax.shard_map(body, mesh=mesh, in_specs=in_specs, out_specs=out_specs, check_vma=False)
```

```python
import functools
import math

import jax
import jax.numpy as jnp
from jax import lax
from jax.experimental import pallas as pl
from jax.experimental.pallas import tpu as pltpu
from jax.sharding import PartitionSpec as P

MESH = pl.DeviceIdType.MESH
POOL = 8
CHIPS = 8
CORES = 2
LAYERS = 4
LIST = 12
SLOTS = 64
TOK = 8
CAP = 2
ROWS = CAP * TOK
HEADS = 8
HD = 128
QH = 8
SPAN = 256
ENTRIES = 8
DISTANCE = (4, 3, 5, 2, 6, 1, 7)
FIRST_FAR = 2
SOURCES = FIRST_FAR + len(DISTANCE)
GROUPS = ((0, 2), (2, 3), (3, 5), (5, 7), (7, 9))
N_GROUPS = len(GROUPS)
KEYS = CORES * CHIPS * ROWS
MASKED = -1e30
SPREAD_AHEAD = 4
SHARE_AHEAD = 2
TO_LOG2 = math.log2(math.e) / math.sqrt(HD)


def interleave(first, second):
    first = first.astype(jnp.float32)
    second = second.astype(jnp.float32)
    pieces = []
    for head in range(HEADS):
        rows = slice(head * TOK, (head + 1) * TOK)
        pieces += [first[rows], second[rows]]
    return jnp.concatenate(pieces, axis=0).astype(jnp.bfloat16)


def kernel(
    ids_in, counts_in, new_ids_in, q_in, cache_in, new_in, attn_out, stored_out,
    ids, counts, new_ids,
    cache, new, q, zsend, zbuf, kv, nsend, nrecv, placed, attn, top, total, acc, qt, flipped, causal,
    in_sem, zs, zr, ps, pr, ss, sr, ns, nr, out_sem,
):
    pool = lax.axis_index("pool")
    tp = lax.axis_index("tp")
    core = lax.rem(tp, CORES)
    chip = lax.div(tp, CORES)

    def pool_peer(distance):
        return lax.rem(pool + distance, POOL)

    def chip_peer(step):
        return lax.rem(chip + step, CHIPS)

    sibling = {"tp": chip * CORES + 1 - core}

    moves = ((ids_in, ids), (counts_in, counts), (new_ids_in, new_ids), (cache_in, cache), (new_in, new), (q_in, q))
    loads = [pltpu.make_async_copy(*move, in_sem.at[index]) for index, move in enumerate(moves)]
    for load in loads:
        load.start()

    barrier = pltpu.get_barrier_semaphore()
    for distance in DISTANCE:
        pl.semaphore_signal(barrier, inc=1, device_id={"pool": pool_peer(distance)}, device_id_type=MESH)
    for step in range(1, CHIPS):
        pl.semaphore_signal(
            barrier, inc=1, device_id={"tp": chip_peer(step) * CORES + core}, device_id_type=MESH
        )
    pl.semaphore_signal(barrier, inc=1, device_id=sibling, device_id_type=MESH)

    def prepare(layer):
        for place in range(FIRST_FAR - 1, SOURCES):
            distance = 0 if place < FIRST_FAR else DISTANCE[place - FIRST_FAR]
            prompt = pool_peer(distance)
            live = counts[0, prompt]
            first = jnp.int32(0)
            last = jnp.int32(0)
            found = [
                ((ids[prompt, layer, j] >> 6) == pool) & (j < live) for j in range(LIST)
            ]
            slot = [ids[prompt, layer, j] & (SLOTS - 1) for j in range(LIST)]
            for j in range(LIST):
                last = jnp.where(found[j], slot[j], last)
                first = jnp.where(found[LIST - 1 - j], slot[LIST - 1 - j], first)
            rows = interleave(cache[first], cache[last])
            if place < FIRST_FAR:
                zbuf[layer, place] = rows
            else:
                zsend[layer, place - FIRST_FAR] = rows
        zbuf[layer, 0] = interleave(new[2 * layer], new[2 * layer + 1])

    def z_copy(layer, index):
        return pltpu.make_async_remote_copy(
            src_ref=zsend.at[layer, index],
            dst_ref=zbuf.at[layer, FIRST_FAR + index],
            send_sem=zs.at[layer],
            recv_sem=zr.at[layer, index],
            device_id={"pool": pool_peer(DISTANCE[index])},
            device_id_type=MESH,
        )

    def n_copy(index):
        return pltpu.make_async_remote_copy(
            src_ref=nsend.at[index],
            dst_ref=nrecv.at[1 + index],
            send_sem=ns.at[0],
            recv_sem=nr.at[0],
            device_id={"pool": pool_peer(DISTANCE[index])},
            device_id_type=MESH,
        )

    def whole(part, send_sem, recv_sem):
        return pltpu.make_async_remote_copy(
            src_ref=part,
            dst_ref=part,
            send_sem=send_sem,
            recv_sem=recv_sem,
            device_id=sibling,
            device_id_type=MESH,
        )

    def plane_copy(layer, group, step):
        low, high = GROUPS[group]
        target = chip_peer(step)
        return pltpu.make_async_remote_copy(
            src_ref=zbuf.at[layer, pl.ds(low, high - low), pl.ds(pl.multiple_of(target * ROWS, ROWS), ROWS)],
            dst_ref=kv.at[
                layer,
                pl.ds(low, high - low),
                pl.ds(pl.multiple_of((core * CHIPS + chip) * ROWS, ROWS), ROWS),
            ],
            send_sem=ps.at[layer, group],
            recv_sem=pr.at[layer, group],
            device_id={"tp": target * CORES + core},
            device_id_type=MESH,
        )

    def plane_copies(layer, group):
        low, high = GROUPS[group]
        part = zbuf.at[layer, pl.ds(low, high - low), pl.ds(0, (CHIPS - 1) * ROWS)]
        return whole(part, ps.at[layer, group], pr.at[layer, group])

    def sibling_copy(layer, group):
        low, high = GROUPS[group]
        half = (
            layer,
            pl.ds(low, high - low),
            pl.ds(pl.multiple_of(core * CHIPS * ROWS, CHIPS * ROWS), CHIPS * ROWS),
        )
        return pltpu.make_async_remote_copy(
            src_ref=kv.at[half],
            dst_ref=kv.at[half],
            send_sem=ss.at[layer, group],
            recv_sem=sr.at[layer, group],
            device_id=sibling,
            device_id_type=MESH,
        )

    def spread(layer, group):
        low, high = GROUPS[group]
        for place in range(max(low, FIRST_FAR), high):
            z_copy(layer, place - FIRST_FAR).wait_recv()
        for step in range(1, CHIPS):
            plane_copy(layer, group, step).start()
        mine = zbuf[layer, pl.ds(low, high - low), pl.ds(pl.multiple_of(chip * ROWS, ROWS), ROWS)]
        kv[
            layer,
            pl.ds(low, high - low),
            pl.ds(pl.multiple_of((core * CHIPS + chip) * ROWS, ROWS), ROWS),
        ] = mine

    def share(layer, group):
        plane_copies(layer, group).wait_recv()
        sibling_copy(layer, group).start()

    def attend(layer, group):
        low, high = GROUPS[group]
        count = high - low
        sibling_copy(layer, group).wait_recv()
        biases = []
        for place in range(low, high):
            if place == 0:
                biases.append(None)
                continue
            distance = 0 if place < FIRST_FAR else DISTANCE[place - FIRST_FAR]
            holder = lax.rem(pool + POOL - distance, POOL)
            live = counts[0, pool]
            named = jnp.int32(0)
            for j in range(LIST):
                hit = ((ids[pool, layer, j] >> 6) == holder) & (j < live)
                named += jnp.where(hit, 1, 0)
            biases.append([jnp.where(slot < named, 0.0, MASKED) for slot in range(CAP)])
        for index in range(count):
            values = kv[layer, low + index, :, HD:].astype(jnp.float32)
            flipped[:, index * KEYS : (index + 1) * KEYS] = values.T.astype(jnp.bfloat16)

        def score(head):
            rows = qt[layer, head]
            scores = []
            for index in range(count):
                block = jnp.dot(
                    kv[layer, low + index, :, :HD], rows, preferred_element_type=jnp.float32
                )
                if biases[index] is None:
                    block = block + causal[...]
                scores.append(block.reshape(KEYS // ROWS, CAP, TOK, SPAN))
            return scores

        def weigh(head, scores):
            highest = None
            for block, bias in zip(scores, biases):
                peak = jnp.max(block, axis=0)
                if bias is None:
                    peak = jnp.maximum(peak[0], peak[1])
                else:
                    peak = jnp.maximum(peak[0] + bias[0], peak[1] + bias[1])
                highest = peak if highest is None else jnp.maximum(highest, peak)
            highest = jnp.max(highest, axis=0, keepdims=True) * TO_LOG2
            shrink = None
            if group > 0:
                before = top[layer, head]
                highest = jnp.maximum(highest, before)
                shrink = jnp.exp2(before - highest)
            weights = []
            added = None
            for block, bias in zip(scores, biases):
                shifts = [highest] * CAP if bias is None else [highest - x for x in bias]
                shift = jnp.stack([jnp.broadcast_to(x, (TOK, SPAN)) for x in shifts])
                weight = jnp.exp2(block * TO_LOG2 - shift[None])
                part = jnp.sum(weight, axis=(0, 1))
                added = part if added is None else added + part
                weights.append(weight.reshape(KEYS, SPAN).astype(jnp.bfloat16))
            weights = jnp.concatenate(weights, axis=0) if count > 1 else weights[0]
            added = jnp.sum(added, axis=0, keepdims=True)
            if group > 0:
                added = added + shrink * total[layer, head]
            total[layer, head] = added
            top[layer, head] = highest
            return weights, shrink

        def mix(head, weights, shrink):
            mixed = jnp.dot(
                flipped[:, : count * KEYS], weights, preferred_element_type=jnp.float32
            )
            if group > 0:
                mixed = mixed + shrink * acc[layer, head]
            if group < N_GROUPS - 1:
                acc[layer, head] = mixed
            else:
                attn[layer, :, head * HD : (head + 1) * HD] = (mixed / total[layer, head]).T.astype(jnp.bfloat16)

        scores = [score(head) for head in range(QH)]
        weights = [weigh(head, scores[head]) for head in range(QH)]
        for head in range(QH):
            mix(head, *weights[head])

    def attn_copy(layer):
        return pltpu.make_async_copy(attn.at[layer], attn_out.at[layer], out_sem.at[layer])

    for load in loads[:5]:
        load.wait()
    prepare(0)
    pl.semaphore_wait(barrier, len(DISTANCE) + CHIPS)
    def send(layer):
        spread(layer, 0)
        for index in range(len(DISTANCE)):
            z_copy(layer, index).start()

    send(0)

    @pl.loop(1, LAYERS)
    def _(layer):
        prepare(layer)
        send(layer)

    for place in range(POOL):
        distance = 0 if place == 0 else DISTANCE[place - 1]
        holder = pool_peer(distance)
        entry = jnp.int32(0)
        for e in range(ENTRIES):
            entry = jnp.where((new_ids[e // 2, e % 2, pool] >> 3) == holder, e, entry)
        if place == 0:
            nrecv[0] = new[entry]
        else:
            nsend[place - 1] = new[entry]
    origin = [jnp.int32(0)] * ENTRIES
    for place in range(POOL):
        distance = 0 if place == 0 else DISTANCE[place - 1]
        prompt = lax.rem(pool + POOL - distance, POOL)
        slot = jnp.int32(0)
        for e in range(ENTRIES):
            written = new_ids[e // 2, e % 2, prompt]
            slot = jnp.where((written >> 3) == pool, written & 7, slot)
        origin = [jnp.where(slot == j, place, origin[j]) for j in range(ENTRIES)]

    row = lax.broadcasted_iota(jnp.int32, (KEYS, SPAN), 0)
    position = ((row >> 3) & 1) * 128 + (((row >> 4) & 7) * 2 + (row >> 7)) * TOK + (row & 7)
    query = lax.broadcasted_iota(jnp.int32, (KEYS, SPAN), 1)
    causal[...] = jnp.where(position <= query, 0.0, MASKED)
    loads[5].wait()

    def turn(layer):
        for head in range(QH):
            columns = slice(head * HD, (head + 1) * HD)
            qt[layer, head] = q[layer, :, columns].astype(jnp.float32).T.astype(jnp.bfloat16)

    @pl.loop(0, LAYERS)
    def _(layer):
        turn(layer)
        share(layer, 0)

    @pl.loop(0, LAYERS)
    def _(layer):
        attend(layer, 0)
        for step in range(SPREAD_AHEAD):

            @pl.when(layer == min(1 + step // 2, LAYERS - 1))
            def _():
                spread(0, 1 + step)

        for step in range(SHARE_AHEAD):

            @pl.when(layer == min(2 + step, LAYERS - 1))
            def _():
                share(0, 1 + step)

    def ahead(layer, group, steps, stage):
        later, group = divmod(group - 1 + steps, N_GROUPS - 1)
        if later == 0:
            stage(layer, group + 1)
        else:

            @pl.when(layer + later < LAYERS)
            def _():
                stage(layer + later, group + 1)

    last = divmod(N_GROUPS - 2 - SPREAD_AHEAD, N_GROUPS - 1)

    @pl.loop(0, LAYERS)
    def _(layer):
        for group in range(1, N_GROUPS):
            ahead(layer, group, SPREAD_AHEAD, spread)
            if group - 1 == last[1]:

                @pl.when(layer == LAYERS - 1 + last[0])
                def _():
                    for index in range(len(DISTANCE)):
                        n_copy(index).start()

            attend(layer, group)
            ahead(layer, group, SHARE_AHEAD, share)
        attn_copy(layer).start()

    whole(nsend, ns.at[0], nr.at[0]).wait_recv()
    for j in range(ENTRIES):
        placed[j] = nrecv[origin[j]]
    stored_copy = pltpu.make_async_copy(placed, stored_out, out_sem.at[LAYERS])
    stored_copy.start()

    @pl.loop(0, LAYERS)
    def _(layer):
        whole(zsend.at[layer], zs.at[layer], zr.at[layer, 0]).wait_send()
        for group in range(N_GROUPS):
            plane_copies(layer, group).wait_send()
            sibling_copy(layer, group).wait_send()
        attn_copy(layer).wait()

    whole(nsend, ns.at[0], nr.at[0]).wait_send()
    stored_copy.wait()


def body(queries, pool_cache, new_kv, block_ids, prefix_count, new_ids):
    hbm = pl.BlockSpec(memory_space=pltpu.HBM)
    anywhere = pl.BlockSpec(memory_space=pl.ANY)
    bf16 = jnp.bfloat16
    far = len(DISTANCE)
    attn, stored = pl.pallas_call(
        kernel,
        out_shape=(
            jax.ShapeDtypeStruct((LAYERS, SPAN, QH * HD), bf16),
            jax.ShapeDtypeStruct((ENTRIES, HEADS * TOK, 2 * HD), bf16),
        ),
        in_specs=[hbm] * 6,
        out_specs=(anywhere, anywhere),
        scratch_shapes=[
            pltpu.SMEM((POOL, LAYERS, LIST), jnp.int32),
            pltpu.SMEM((1, POOL), jnp.int32),
            pltpu.SMEM((LAYERS, ENTRIES // LAYERS, POOL), jnp.int32),
            pltpu.VMEM((SLOTS, HEADS * TOK, 2 * HD), bf16),
            pltpu.VMEM((ENTRIES, HEADS * TOK, 2 * HD), bf16),
            pltpu.VMEM((LAYERS, SPAN, QH * HD), bf16),
            pltpu.VMEM((LAYERS, far, HEADS * ROWS, 2 * HD), bf16),
            pltpu.VMEM((LAYERS, SOURCES, HEADS * ROWS, 2 * HD), bf16),
            pltpu.VMEM((LAYERS, SOURCES, CORES * CHIPS * ROWS, 2 * HD), bf16),
            pltpu.VMEM((far, HEADS * TOK, 2 * HD), bf16),
            pltpu.VMEM((POOL, HEADS * TOK, 2 * HD), bf16),
            pltpu.VMEM((ENTRIES, HEADS * TOK, 2 * HD), bf16),
            pltpu.VMEM((LAYERS, SPAN, QH * HD), bf16),
            pltpu.VMEM((LAYERS, QH, 1, SPAN), jnp.float32),
            pltpu.VMEM((LAYERS, QH, 1, SPAN), jnp.float32),
            pltpu.VMEM((LAYERS, QH, HD, SPAN), jnp.float32),
            pltpu.VMEM((LAYERS, QH, HD, SPAN), bf16),
            pltpu.VMEM((HD, max(high - low for low, high in GROUPS) * KEYS), bf16),
            pltpu.VMEM((KEYS, SPAN), jnp.float32),
            pltpu.SemaphoreType.DMA((6,)),
            pltpu.SemaphoreType.DMA((LAYERS,)),
            pltpu.SemaphoreType.DMA((LAYERS, far)),
            pltpu.SemaphoreType.DMA((LAYERS, N_GROUPS)),
            pltpu.SemaphoreType.DMA((LAYERS, N_GROUPS)),
            pltpu.SemaphoreType.DMA((LAYERS, N_GROUPS)),
            pltpu.SemaphoreType.DMA((LAYERS, N_GROUPS)),
            pltpu.SemaphoreType.DMA((1,)),
            pltpu.SemaphoreType.DMA((1,)),
            pltpu.SemaphoreType.DMA((LAYERS + 1,)),
        ],
        compiler_params=pltpu.CompilerParams(
            collective_id=0, has_side_effects=True, vmem_limit_bytes=60 << 20
        ),
    )(
        block_ids[0],
        prefix_count,
        new_ids[0].transpose(1, 2, 0),
        queries[0, 0],
        pool_cache.reshape(SLOTS, HEADS * TOK, 2 * HD),
        new_kv.reshape(ENTRIES, HEADS * TOK, 2 * HD),
    )
    return attn[None, None], stored.reshape(1, ENTRIES, HEADS, TOK, 2 * HD)


def solution(mesh):
    in_specs = (
        P("rep", "pool", None, None, "tp"),
        P("pool", None, "tp", None),
        P("rep", "pool", None, None, None, "tp", None),
        P("rep", None, None, None),
        P("rep", None),
        P("rep", None, None, None),
    )
    out_specs = (P("rep", "pool", None, None, "tp"), P("rep", "pool", None, "tp", None))
    return jax.shard_map(body, mesh=mesh, in_specs=in_specs, out_specs=out_specs, check_vma=False)
```

```python
import functools
import math

import jax
import jax.numpy as jnp
from jax import lax
from jax.experimental import pallas as pl
from jax.experimental.pallas import tpu as pltpu
from jax.sharding import PartitionSpec as P

MESH = pl.DeviceIdType.MESH
POOL = 8
CHIPS = 8
CORES = 2
LAYERS = 4
LIST = 12
SLOTS = 64
TOK = 8
CAP = 2
ROWS = CAP * TOK
HEADS = 8
HD = 128
QH = 8
SPAN = 256
ENTRIES = 8
DISTANCE = (3, 5, 2, 6, 1, 7, 4)
FIRST_FAR = 2
SOURCES = FIRST_FAR + len(DISTANCE)
GROUPS = ((0, 2), (2, 4), (4, 6), (6, 8), (8, 9))
N_GROUPS = len(GROUPS)
KEYS = CORES * CHIPS * ROWS
MASKED = -1e30
SPREAD_AHEAD = 4
SHARE_AHEAD = 2
TO_LOG2 = math.log2(math.e) / math.sqrt(HD)


def interleave(first, second):
    first = first.astype(jnp.float32)
    second = second.astype(jnp.float32)
    pieces = []
    for head in range(HEADS):
        rows = slice(head * TOK, (head + 1) * TOK)
        pieces += [first[rows], second[rows]]
    return jnp.concatenate(pieces, axis=0).astype(jnp.bfloat16)


def kernel(
    ids_in, counts_in, new_ids_in, q_in, cache_in, new_in, attn_out, stored_out,
    ids, counts, new_ids,
    cache, new, q, zsend, zbuf, kv, nsend, nrecv, placed, attn, top, total, acc, qt, flipped, causal,
    in_sem, zs, zr, ps, pr, ss, sr, ns, nr, out_sem,
):
    pool = lax.axis_index("pool")
    tp = lax.axis_index("tp")
    core = lax.rem(tp, CORES)
    chip = lax.div(tp, CORES)

    def pool_peer(distance):
        return lax.rem(pool + distance, POOL)

    def chip_peer(step):
        return lax.rem(chip + step, CHIPS)

    sibling = {"tp": chip * CORES + 1 - core}

    moves = ((ids_in, ids), (counts_in, counts), (new_ids_in, new_ids), (cache_in, cache), (new_in, new), (q_in, q))
    loads = [pltpu.make_async_copy(*move, in_sem.at[index]) for index, move in enumerate(moves)]
    for load in loads:
        load.start()

    barrier = pltpu.get_barrier_semaphore()
    for distance in DISTANCE:
        pl.semaphore_signal(barrier, inc=1, device_id={"pool": pool_peer(distance)}, device_id_type=MESH)
    for step in range(1, CHIPS):
        pl.semaphore_signal(
            barrier, inc=1, device_id={"tp": chip_peer(step) * CORES + core}, device_id_type=MESH
        )
    pl.semaphore_signal(barrier, inc=1, device_id=sibling, device_id_type=MESH)

    def prepare(layer):
        for place in range(FIRST_FAR - 1, SOURCES):
            distance = 0 if place < FIRST_FAR else DISTANCE[place - FIRST_FAR]
            prompt = pool_peer(distance)
            live = counts[0, prompt]
            first = jnp.int32(0)
            last = jnp.int32(0)
            found = [
                ((ids[prompt, layer, j] >> 6) == pool) & (j < live) for j in range(LIST)
            ]
            slot = [ids[prompt, layer, j] & (SLOTS - 1) for j in range(LIST)]
            for j in range(LIST):
                last = jnp.where(found[j], slot[j], last)
                first = jnp.where(found[LIST - 1 - j], slot[LIST - 1 - j], first)
            rows = interleave(cache[first], cache[last])
            if place < FIRST_FAR:
                zbuf[layer, place] = rows
            else:
                zsend[layer, place - FIRST_FAR] = rows
        zbuf[layer, 0] = interleave(new[2 * layer], new[2 * layer + 1])

    def z_copy(layer, index):
        return pltpu.make_async_remote_copy(
            src_ref=zsend.at[layer, index],
            dst_ref=zbuf.at[layer, FIRST_FAR + index],
            send_sem=zs.at[layer],
            recv_sem=zr.at[layer, index],
            device_id={"pool": pool_peer(DISTANCE[index])},
            device_id_type=MESH,
        )

    def n_copy(index):
        return pltpu.make_async_remote_copy(
            src_ref=nsend.at[index],
            dst_ref=nrecv.at[1 + index],
            send_sem=ns.at[0],
            recv_sem=nr.at[0],
            device_id={"pool": pool_peer(DISTANCE[index])},
            device_id_type=MESH,
        )

    def whole(part, send_sem, recv_sem):
        return pltpu.make_async_remote_copy(
            src_ref=part,
            dst_ref=part,
            send_sem=send_sem,
            recv_sem=recv_sem,
            device_id=sibling,
            device_id_type=MESH,
        )

    def plane_copy(layer, group, step):
        low, high = GROUPS[group]
        target = chip_peer(step)
        return pltpu.make_async_remote_copy(
            src_ref=zbuf.at[layer, pl.ds(low, high - low), pl.ds(pl.multiple_of(target * ROWS, ROWS), ROWS)],
            dst_ref=kv.at[
                layer,
                pl.ds(low, high - low),
                pl.ds(pl.multiple_of((core * CHIPS + chip) * ROWS, ROWS), ROWS),
            ],
            send_sem=ps.at[layer, group],
            recv_sem=pr.at[layer, group],
            device_id={"tp": target * CORES + core},
            device_id_type=MESH,
        )

    def plane_copies(layer, group):
        low, high = GROUPS[group]
        part = zbuf.at[layer, pl.ds(low, high - low), pl.ds(0, (CHIPS - 1) * ROWS)]
        return whole(part, ps.at[layer, group], pr.at[layer, group])

    def sibling_copy(layer, group):
        low, high = GROUPS[group]
        half = (
            layer,
            pl.ds(low, high - low),
            pl.ds(pl.multiple_of(core * CHIPS * ROWS, CHIPS * ROWS), CHIPS * ROWS),
        )
        return pltpu.make_async_remote_copy(
            src_ref=kv.at[half],
            dst_ref=kv.at[half],
            send_sem=ss.at[layer, group],
            recv_sem=sr.at[layer, group],
            device_id=sibling,
            device_id_type=MESH,
        )

    def spread(layer, group):
        low, high = GROUPS[group]
        for place in range(max(low, FIRST_FAR), high):
            z_copy(layer, place - FIRST_FAR).wait_recv()
        for step in range(1, CHIPS):
            plane_copy(layer, group, step).start()
        mine = zbuf[layer, pl.ds(low, high - low), pl.ds(pl.multiple_of(chip * ROWS, ROWS), ROWS)]
        kv[
            layer,
            pl.ds(low, high - low),
            pl.ds(pl.multiple_of((core * CHIPS + chip) * ROWS, ROWS), ROWS),
        ] = mine

    def share(layer, group):
        plane_copies(layer, group).wait_recv()
        sibling_copy(layer, group).start()

    def attend(layer, group):
        low, high = GROUPS[group]
        count = high - low
        sibling_copy(layer, group).wait_recv()
        biases = []
        for place in range(low, high):
            if place == 0:
                biases.append(None)
                continue
            distance = 0 if place < FIRST_FAR else DISTANCE[place - FIRST_FAR]
            holder = lax.rem(pool + POOL - distance, POOL)
            live = counts[0, pool]
            named = jnp.int32(0)
            for j in range(LIST):
                hit = ((ids[pool, layer, j] >> 6) == holder) & (j < live)
                named += jnp.where(hit, 1, 0)
            biases.append([jnp.where(slot < named, 0.0, MASKED) for slot in range(CAP)])
        for index in range(count):
            values = kv[layer, low + index, :, HD:].astype(jnp.float32)
            flipped[:, index * KEYS : (index + 1) * KEYS] = values.T.astype(jnp.bfloat16)

        def score(head):
            rows = qt[layer, head]
            scores = []
            for index in range(count):
                block = jnp.dot(
                    kv[layer, low + index, :, :HD], rows, preferred_element_type=jnp.float32
                )
                if biases[index] is None:
                    block = block + causal[...]
                scores.append(block.reshape(KEYS // ROWS, CAP, TOK, SPAN))
            return scores

        def weigh(head, scores):
            highest = None
            for block, bias in zip(scores, biases):
                peak = jnp.max(block, axis=0)
                if bias is None:
                    peak = jnp.maximum(peak[0], peak[1])
                else:
                    peak = jnp.maximum(peak[0] + bias[0], peak[1] + bias[1])
                highest = peak if highest is None else jnp.maximum(highest, peak)
            highest = jnp.max(highest, axis=0, keepdims=True) * TO_LOG2
            shrink = None
            if group > 0:
                before = top[layer, head]
                highest = jnp.maximum(highest, before)
                shrink = jnp.exp2(before - highest)
            weights = []
            added = None
            for block, bias in zip(scores, biases):
                shifts = [highest] * CAP if bias is None else [highest - x for x in bias]
                shift = jnp.stack([jnp.broadcast_to(x, (TOK, SPAN)) for x in shifts])
                weight = jnp.exp2(block * TO_LOG2 - shift[None])
                part = jnp.sum(weight, axis=(0, 1))
                added = part if added is None else added + part
                weights.append(weight.reshape(KEYS, SPAN).astype(jnp.bfloat16))
            weights = jnp.concatenate(weights, axis=0) if count > 1 else weights[0]
            added = jnp.sum(added, axis=0, keepdims=True)
            if group > 0:
                added = added + shrink * total[layer, head]
            total[layer, head] = added
            top[layer, head] = highest
            return weights, shrink

        def mix(head, weights, shrink):
            mixed = jnp.dot(
                flipped[:, : count * KEYS], weights, preferred_element_type=jnp.float32
            )
            if group > 0:
                mixed = mixed + shrink * acc[layer, head]
            if group < N_GROUPS - 1:
                acc[layer, head] = mixed
            else:
                attn[layer, :, head * HD : (head + 1) * HD] = (mixed / total[layer, head]).T.astype(jnp.bfloat16)

        scores = [score(head) for head in range(QH)]
        weights = [weigh(head, scores[head]) for head in range(QH)]
        for head in range(QH):
            mix(head, *weights[head])

    def attn_copy(layer):
        return pltpu.make_async_copy(attn.at[layer], attn_out.at[layer], out_sem.at[layer])

    for load in loads[:5]:
        load.wait()
    prepare(0)
    pl.semaphore_wait(barrier, len(DISTANCE) + CHIPS)
    def send(layer):
        spread(layer, 0)
        for index in range(len(DISTANCE)):
            z_copy(layer, index).start()

    send(0)

    @pl.loop(1, LAYERS)
    def _(layer):
        prepare(layer)
        send(layer)

    for place in range(POOL):
        distance = 0 if place == 0 else DISTANCE[place - 1]
        holder = pool_peer(distance)
        entry = jnp.int32(0)
        for e in range(ENTRIES):
            entry = jnp.where((new_ids[e // 2, e % 2, pool] >> 3) == holder, e, entry)
        if place == 0:
            nrecv[0] = new[entry]
        else:
            nsend[place - 1] = new[entry]
    origin = [jnp.int32(0)] * ENTRIES
    for place in range(POOL):
        distance = 0 if place == 0 else DISTANCE[place - 1]
        prompt = lax.rem(pool + POOL - distance, POOL)
        slot = jnp.int32(0)
        for e in range(ENTRIES):
            written = new_ids[e // 2, e % 2, prompt]
            slot = jnp.where((written >> 3) == pool, written & 7, slot)
        origin = [jnp.where(slot == j, place, origin[j]) for j in range(ENTRIES)]

    row = lax.broadcasted_iota(jnp.int32, (KEYS, SPAN), 0)
    position = ((row >> 3) & 1) * 128 + (((row >> 4) & 7) * 2 + (row >> 7)) * TOK + (row & 7)
    query = lax.broadcasted_iota(jnp.int32, (KEYS, SPAN), 1)
    causal[...] = jnp.where(position <= query, 0.0, MASKED)
    loads[5].wait()

    def turn(layer):
        for head in range(QH):
            columns = slice(head * HD, (head + 1) * HD)
            qt[layer, head] = q[layer, :, columns].astype(jnp.float32).T.astype(jnp.bfloat16)

    @pl.loop(0, LAYERS)
    def _(layer):
        turn(layer)
        share(layer, 0)

    @pl.loop(0, LAYERS)
    def _(layer):
        attend(layer, 0)
        for step in range(SPREAD_AHEAD):

            @pl.when(layer == min(1 + step // 2, LAYERS - 1))
            def _():
                spread(0, 1 + step)

        for step in range(SHARE_AHEAD):

            @pl.when(layer == min(2 + step, LAYERS - 1))
            def _():
                share(0, 1 + step)

    def ahead(layer, group, steps, stage):
        later, group = divmod(group - 1 + steps, N_GROUPS - 1)
        if later == 0:
            stage(layer, group + 1)
        else:

            @pl.when(layer + later < LAYERS)
            def _():
                stage(layer + later, group + 1)

    last = divmod(N_GROUPS - 2 - SPREAD_AHEAD, N_GROUPS - 1)

    @pl.loop(0, LAYERS)
    def _(layer):
        for group in range(1, N_GROUPS):
            ahead(layer, group, SPREAD_AHEAD, spread)
            if group - 1 == last[1]:

                @pl.when(layer == LAYERS - 1 + last[0])
                def _():
                    for index in range(len(DISTANCE)):
                        n_copy(index).start()

            attend(layer, group)
            ahead(layer, group, SHARE_AHEAD, share)
        attn_copy(layer).start()

    whole(nsend, ns.at[0], nr.at[0]).wait_recv()
    for j in range(ENTRIES):
        placed[j] = nrecv[origin[j]]
    stored_copy = pltpu.make_async_copy(placed, stored_out, out_sem.at[LAYERS])
    stored_copy.start()

    @pl.loop(0, LAYERS)
    def _(layer):
        whole(zsend.at[layer], zs.at[layer], zr.at[layer, 0]).wait_send()
        for group in range(N_GROUPS):
            plane_copies(layer, group).wait_send()
            sibling_copy(layer, group).wait_send()
        attn_copy(layer).wait()

    whole(nsend, ns.at[0], nr.at[0]).wait_send()
    stored_copy.wait()


def body(queries, pool_cache, new_kv, block_ids, prefix_count, new_ids):
    hbm = pl.BlockSpec(memory_space=pltpu.HBM)
    anywhere = pl.BlockSpec(memory_space=pl.ANY)
    bf16 = jnp.bfloat16
    far = len(DISTANCE)
    attn, stored = pl.pallas_call(
        kernel,
        out_shape=(
            jax.ShapeDtypeStruct((LAYERS, SPAN, QH * HD), bf16),
            jax.ShapeDtypeStruct((ENTRIES, HEADS * TOK, 2 * HD), bf16),
        ),
        in_specs=[hbm] * 6,
        out_specs=(anywhere, anywhere),
        scratch_shapes=[
            pltpu.SMEM((POOL, LAYERS, LIST), jnp.int32),
            pltpu.SMEM((1, POOL), jnp.int32),
            pltpu.SMEM((LAYERS, ENTRIES // LAYERS, POOL), jnp.int32),
            pltpu.VMEM((SLOTS, HEADS * TOK, 2 * HD), bf16),
            pltpu.VMEM((ENTRIES, HEADS * TOK, 2 * HD), bf16),
            pltpu.VMEM((LAYERS, SPAN, QH * HD), bf16),
            pltpu.VMEM((LAYERS, far, HEADS * ROWS, 2 * HD), bf16),
            pltpu.VMEM((LAYERS, SOURCES, HEADS * ROWS, 2 * HD), bf16),
            pltpu.VMEM((LAYERS, SOURCES, CORES * CHIPS * ROWS, 2 * HD), bf16),
            pltpu.VMEM((far, HEADS * TOK, 2 * HD), bf16),
            pltpu.VMEM((POOL, HEADS * TOK, 2 * HD), bf16),
            pltpu.VMEM((ENTRIES, HEADS * TOK, 2 * HD), bf16),
            pltpu.VMEM((LAYERS, SPAN, QH * HD), bf16),
            pltpu.VMEM((LAYERS, QH, 1, SPAN), jnp.float32),
            pltpu.VMEM((LAYERS, QH, 1, SPAN), jnp.float32),
            pltpu.VMEM((LAYERS, QH, HD, SPAN), jnp.float32),
            pltpu.VMEM((LAYERS, QH, HD, SPAN), bf16),
            pltpu.VMEM((HD, max(high - low for low, high in GROUPS) * KEYS), bf16),
            pltpu.VMEM((KEYS, SPAN), jnp.float32),
            pltpu.SemaphoreType.DMA((6,)),
            pltpu.SemaphoreType.DMA((LAYERS,)),
            pltpu.SemaphoreType.DMA((LAYERS, far)),
            pltpu.SemaphoreType.DMA((LAYERS, N_GROUPS)),
            pltpu.SemaphoreType.DMA((LAYERS, N_GROUPS)),
            pltpu.SemaphoreType.DMA((LAYERS, N_GROUPS)),
            pltpu.SemaphoreType.DMA((LAYERS, N_GROUPS)),
            pltpu.SemaphoreType.DMA((1,)),
            pltpu.SemaphoreType.DMA((1,)),
            pltpu.SemaphoreType.DMA((LAYERS + 1,)),
        ],
        compiler_params=pltpu.CompilerParams(
            collective_id=0, has_side_effects=True, vmem_limit_bytes=60 << 20
        ),
    )(
        block_ids[0],
        prefix_count,
        new_ids[0].transpose(1, 2, 0),
        queries[0, 0],
        pool_cache.reshape(SLOTS, HEADS * TOK, 2 * HD),
        new_kv.reshape(ENTRIES, HEADS * TOK, 2 * HD),
    )
    return attn[None, None], stored.reshape(1, ENTRIES, HEADS, TOK, 2 * HD)


def solution(mesh):
    in_specs = (
        P("rep", "pool", None, None, "tp"),
        P("pool", None, "tp", None),
        P("rep", "pool", None, None, None, "tp", None),
        P("rep", None, None, None),
        P("rep", None),
        P("rep", None, None, None),
    )
    out_specs = (P("rep", "pool", None, None, "tp"), P("rep", "pool", None, "tp", None))
    return jax.shard_map(body, mesh=mesh, in_specs=in_specs, out_specs=out_specs, check_vma=False)
```

```python
import functools
import math

import jax
import jax.numpy as jnp
from jax import lax
from jax.experimental import pallas as pl
from jax.experimental.pallas import tpu as pltpu
from jax.sharding import PartitionSpec as P

MESH = pl.DeviceIdType.MESH
POOL = 8
CHIPS = 8
CORES = 2
LAYERS = 4
LIST = 12
SLOTS = 64
TOK = 8
CAP = 2
ROWS = CAP * TOK
HEADS = 8
HD = 128
QH = 8
SPAN = 256
ENTRIES = 8
DISTANCE = (3, 5, 2, 6, 1, 7, 4)
FIRST_FAR = 2
SOURCES = FIRST_FAR + len(DISTANCE)
GROUPS = ((0, 2), (2, 4), (4, 6), (6, 8), (8, 9))
N_GROUPS = len(GROUPS)
KEYS = CORES * CHIPS * ROWS
MASKED = -1e30
SPREAD_AHEAD = 4
SHARE_AHEAD = 3
TO_LOG2 = math.log2(math.e) / math.sqrt(HD)


def interleave(first, second):
    first = first.astype(jnp.float32)
    second = second.astype(jnp.float32)
    pieces = []
    for head in range(HEADS):
        rows = slice(head * TOK, (head + 1) * TOK)
        pieces += [first[rows], second[rows]]
    return jnp.concatenate(pieces, axis=0).astype(jnp.bfloat16)


def kernel(
    ids_in, counts_in, new_ids_in, q_in, cache_in, new_in, attn_out, stored_out,
    ids, counts, new_ids,
    cache, new, q, zsend, zbuf, kv, nsend, nrecv, placed, attn, top, total, acc, qt, flipped, causal,
    in_sem, zs, zr, ps, pr, ss, sr, ns, nr, out_sem,
):
    pool = lax.axis_index("pool")
    tp = lax.axis_index("tp")
    core = lax.rem(tp, CORES)
    chip = lax.div(tp, CORES)

    def pool_peer(distance):
        return lax.rem(pool + distance, POOL)

    def chip_peer(step):
        return lax.rem(chip + step, CHIPS)

    sibling = {"tp": chip * CORES + 1 - core}

    moves = ((ids_in, ids), (counts_in, counts), (new_ids_in, new_ids), (cache_in, cache), (new_in, new), (q_in, q))
    loads = [pltpu.make_async_copy(*move, in_sem.at[index]) for index, move in enumerate(moves)]
    for load in loads:
        load.start()

    barrier = pltpu.get_barrier_semaphore()
    for distance in DISTANCE:
        pl.semaphore_signal(barrier, inc=1, device_id={"pool": pool_peer(distance)}, device_id_type=MESH)
    for step in range(1, CHIPS):
        pl.semaphore_signal(
            barrier, inc=1, device_id={"tp": chip_peer(step) * CORES + core}, device_id_type=MESH
        )
    pl.semaphore_signal(barrier, inc=1, device_id=sibling, device_id_type=MESH)

    def prepare(layer):
        for place in range(FIRST_FAR - 1, SOURCES):
            distance = 0 if place < FIRST_FAR else DISTANCE[place - FIRST_FAR]
            prompt = pool_peer(distance)
            live = counts[0, prompt]
            first = jnp.int32(0)
            last = jnp.int32(0)
            found = [
                ((ids[prompt, layer, j] >> 6) == pool) & (j < live) for j in range(LIST)
            ]
            slot = [ids[prompt, layer, j] & (SLOTS - 1) for j in range(LIST)]
            for j in range(LIST):
                last = jnp.where(found[j], slot[j], last)
                first = jnp.where(found[LIST - 1 - j], slot[LIST - 1 - j], first)
            rows = interleave(cache[first], cache[last])
            if place < FIRST_FAR:
                zbuf[layer, place] = rows
            else:
                zsend[layer, place - FIRST_FAR] = rows
        zbuf[layer, 0] = interleave(new[2 * layer], new[2 * layer + 1])

    def z_copy(layer, index):
        return pltpu.make_async_remote_copy(
            src_ref=zsend.at[layer, index],
            dst_ref=zbuf.at[layer, FIRST_FAR + index],
            send_sem=zs.at[layer],
            recv_sem=zr.at[layer, index],
            device_id={"pool": pool_peer(DISTANCE[index])},
            device_id_type=MESH,
        )

    def n_copy(index):
        return pltpu.make_async_remote_copy(
            src_ref=nsend.at[index],
            dst_ref=nrecv.at[1 + index],
            send_sem=ns.at[0],
            recv_sem=nr.at[0],
            device_id={"pool": pool_peer(DISTANCE[index])},
            device_id_type=MESH,
        )

    def whole(part, send_sem, recv_sem):
        return pltpu.make_async_remote_copy(
            src_ref=part,
            dst_ref=part,
            send_sem=send_sem,
            recv_sem=recv_sem,
            device_id=sibling,
            device_id_type=MESH,
        )

    def plane_copy(layer, group, step):
        low, high = GROUPS[group]
        target = chip_peer(step)
        return pltpu.make_async_remote_copy(
            src_ref=zbuf.at[layer, pl.ds(low, high - low), pl.ds(pl.multiple_of(target * ROWS, ROWS), ROWS)],
            dst_ref=kv.at[
                layer,
                pl.ds(low, high - low),
                pl.ds(pl.multiple_of((core * CHIPS + chip) * ROWS, ROWS), ROWS),
            ],
            send_sem=ps.at[layer, group],
            recv_sem=pr.at[layer, group],
            device_id={"tp": target * CORES + core},
            device_id_type=MESH,
        )

    def plane_copies(layer, group):
        low, high = GROUPS[group]
        part = zbuf.at[layer, pl.ds(low, high - low), pl.ds(0, (CHIPS - 1) * ROWS)]
        return whole(part, ps.at[layer, group], pr.at[layer, group])

    def sibling_copy(layer, group):
        low, high = GROUPS[group]
        half = (
            layer,
            pl.ds(low, high - low),
            pl.ds(pl.multiple_of(core * CHIPS * ROWS, CHIPS * ROWS), CHIPS * ROWS),
        )
        return pltpu.make_async_remote_copy(
            src_ref=kv.at[half],
            dst_ref=kv.at[half],
            send_sem=ss.at[layer, group],
            recv_sem=sr.at[layer, group],
            device_id=sibling,
            device_id_type=MESH,
        )

    def spread(layer, group):
        low, high = GROUPS[group]
        for place in range(max(low, FIRST_FAR), high):
            z_copy(layer, place - FIRST_FAR).wait_recv()
        for step in range(1, CHIPS):
            plane_copy(layer, group, step).start()
        mine = zbuf[layer, pl.ds(low, high - low), pl.ds(pl.multiple_of(chip * ROWS, ROWS), ROWS)]
        kv[
            layer,
            pl.ds(low, high - low),
            pl.ds(pl.multiple_of((core * CHIPS + chip) * ROWS, ROWS), ROWS),
        ] = mine

    def share(layer, group):
        plane_copies(layer, group).wait_recv()
        sibling_copy(layer, group).start()

    def attend(layer, group):
        low, high = GROUPS[group]
        count = high - low
        sibling_copy(layer, group).wait_recv()
        biases = []
        for place in range(low, high):
            if place == 0:
                biases.append(None)
                continue
            distance = 0 if place < FIRST_FAR else DISTANCE[place - FIRST_FAR]
            holder = lax.rem(pool + POOL - distance, POOL)
            live = counts[0, pool]
            named = jnp.int32(0)
            for j in range(LIST):
                hit = ((ids[pool, layer, j] >> 6) == holder) & (j < live)
                named += jnp.where(hit, 1, 0)
            biases.append([jnp.where(slot < named, 0.0, MASKED) for slot in range(CAP)])
        for index in range(count):
            values = kv[layer, low + index, :, HD:].astype(jnp.float32)
            flipped[:, index * KEYS : (index + 1) * KEYS] = values.T.astype(jnp.bfloat16)

        def score(head):
            rows = qt[layer, head]
            scores = []
            for index in range(count):
                block = jnp.dot(
                    kv[layer, low + index, :, :HD], rows, preferred_element_type=jnp.float32
                )
                if biases[index] is None:
                    block = block + causal[...]
                scores.append(block.reshape(KEYS // ROWS, CAP, TOK, SPAN))
            return scores

        def weigh(head, scores):
            highest = None
            for block, bias in zip(scores, biases):
                peak = jnp.max(block, axis=0)
                if bias is None:
                    peak = jnp.maximum(peak[0], peak[1])
                else:
                    peak = jnp.maximum(peak[0] + bias[0], peak[1] + bias[1])
                highest = peak if highest is None else jnp.maximum(highest, peak)
            highest = jnp.max(highest, axis=0, keepdims=True) * TO_LOG2
            shrink = None
            if group > 0:
                before = top[layer, head]
                highest = jnp.maximum(highest, before)
                shrink = jnp.exp2(before - highest)
            weights = []
            added = None
            for block, bias in zip(scores, biases):
                shifts = [highest] * CAP if bias is None else [highest - x for x in bias]
                shift = jnp.stack([jnp.broadcast_to(x, (TOK, SPAN)) for x in shifts])
                weight = jnp.exp2(block * TO_LOG2 - shift[None])
                part = jnp.sum(weight, axis=(0, 1))
                added = part if added is None else added + part
                weights.append(weight.reshape(KEYS, SPAN).astype(jnp.bfloat16))
            weights = jnp.concatenate(weights, axis=0) if count > 1 else weights[0]
            added = jnp.sum(added, axis=0, keepdims=True)
            if group > 0:
                added = added + shrink * total[layer, head]
            total[layer, head] = added
            top[layer, head] = highest
            return weights, shrink

        def mix(head, weights, shrink):
            mixed = jnp.dot(
                flipped[:, : count * KEYS], weights, preferred_element_type=jnp.float32
            )
            if group > 0:
                mixed = mixed + shrink * acc[layer, head]
            if group < N_GROUPS - 1:
                acc[layer, head] = mixed
            else:
                attn[layer, :, head * HD : (head + 1) * HD] = (mixed / total[layer, head]).T.astype(jnp.bfloat16)

        scores = [score(head) for head in range(QH)]
        weights = [weigh(head, scores[head]) for head in range(QH)]
        for head in range(QH):
            mix(head, *weights[head])

    def attn_copy(layer):
        return pltpu.make_async_copy(attn.at[layer], attn_out.at[layer], out_sem.at[layer])

    for load in loads[:5]:
        load.wait()
    prepare(0)
    pl.semaphore_wait(barrier, len(DISTANCE) + CHIPS)
    def send(layer):
        spread(layer, 0)
        for index in range(len(DISTANCE)):
            z_copy(layer, index).start()

    send(0)

    @pl.loop(1, LAYERS)
    def _(layer):
        prepare(layer)
        send(layer)

    for place in range(POOL):
        distance = 0 if place == 0 else DISTANCE[place - 1]
        holder = pool_peer(distance)
        entry = jnp.int32(0)
        for e in range(ENTRIES):
            entry = jnp.where((new_ids[e // 2, e % 2, pool] >> 3) == holder, e, entry)
        if place == 0:
            nrecv[0] = new[entry]
        else:
            nsend[place - 1] = new[entry]
    origin = [jnp.int32(0)] * ENTRIES
    for place in range(POOL):
        distance = 0 if place == 0 else DISTANCE[place - 1]
        prompt = lax.rem(pool + POOL - distance, POOL)
        slot = jnp.int32(0)
        for e in range(ENTRIES):
            written = new_ids[e // 2, e % 2, prompt]
            slot = jnp.where((written >> 3) == pool, written & 7, slot)
        origin = [jnp.where(slot == j, place, origin[j]) for j in range(ENTRIES)]

    row = lax.broadcasted_iota(jnp.int32, (KEYS, SPAN), 0)
    position = ((row >> 3) & 1) * 128 + (((row >> 4) & 7) * 2 + (row >> 7)) * TOK + (row & 7)
    query = lax.broadcasted_iota(jnp.int32, (KEYS, SPAN), 1)
    causal[...] = jnp.where(position <= query, 0.0, MASKED)
    loads[5].wait()

    def turn(layer):
        for head in range(QH):
            columns = slice(head * HD, (head + 1) * HD)
            qt[layer, head] = q[layer, :, columns].astype(jnp.float32).T.astype(jnp.bfloat16)

    @pl.loop(0, LAYERS)
    def _(layer):
        turn(layer)
        share(layer, 0)

    @pl.loop(0, LAYERS)
    def _(layer):
        attend(layer, 0)
        for step in range(SPREAD_AHEAD):

            @pl.when(layer == min(1 + step // 2, LAYERS - 1))
            def _():
                spread(0, 1 + step)

        for step in range(SHARE_AHEAD):

            @pl.when(layer == min(2 + step, LAYERS - 1))
            def _():
                share(0, 1 + step)

    def ahead(layer, group, steps, stage):
        later, group = divmod(group - 1 + steps, N_GROUPS - 1)
        if later == 0:
            stage(layer, group + 1)
        else:

            @pl.when(layer + later < LAYERS)
            def _():
                stage(layer + later, group + 1)

    last = divmod(N_GROUPS - 2 - SPREAD_AHEAD, N_GROUPS - 1)

    @pl.loop(0, LAYERS)
    def _(layer):
        for group in range(1, N_GROUPS):
            ahead(layer, group, SPREAD_AHEAD, spread)
            if group - 1 == last[1]:

                @pl.when(layer == LAYERS - 1 + last[0])
                def _():
                    for index in range(len(DISTANCE)):
                        n_copy(index).start()

            attend(layer, group)
            ahead(layer, group, SHARE_AHEAD, share)
        attn_copy(layer).start()

    whole(nsend, ns.at[0], nr.at[0]).wait_recv()
    for j in range(ENTRIES):
        placed[j] = nrecv[origin[j]]
    stored_copy = pltpu.make_async_copy(placed, stored_out, out_sem.at[LAYERS])
    stored_copy.start()

    @pl.loop(0, LAYERS)
    def _(layer):
        whole(zsend.at[layer], zs.at[layer], zr.at[layer, 0]).wait_send()
        for group in range(N_GROUPS):
            plane_copies(layer, group).wait_send()
            sibling_copy(layer, group).wait_send()
        attn_copy(layer).wait()

    whole(nsend, ns.at[0], nr.at[0]).wait_send()
    stored_copy.wait()


def body(queries, pool_cache, new_kv, block_ids, prefix_count, new_ids):
    hbm = pl.BlockSpec(memory_space=pltpu.HBM)
    anywhere = pl.BlockSpec(memory_space=pl.ANY)
    bf16 = jnp.bfloat16
    far = len(DISTANCE)
    attn, stored = pl.pallas_call(
        kernel,
        out_shape=(
            jax.ShapeDtypeStruct((LAYERS, SPAN, QH * HD), bf16),
            jax.ShapeDtypeStruct((ENTRIES, HEADS * TOK, 2 * HD), bf16),
        ),
        in_specs=[hbm] * 6,
        out_specs=(anywhere, anywhere),
        scratch_shapes=[
            pltpu.SMEM((POOL, LAYERS, LIST), jnp.int32),
            pltpu.SMEM((1, POOL), jnp.int32),
            pltpu.SMEM((LAYERS, ENTRIES // LAYERS, POOL), jnp.int32),
            pltpu.VMEM((SLOTS, HEADS * TOK, 2 * HD), bf16),
            pltpu.VMEM((ENTRIES, HEADS * TOK, 2 * HD), bf16),
            pltpu.VMEM((LAYERS, SPAN, QH * HD), bf16),
            pltpu.VMEM((LAYERS, far, HEADS * ROWS, 2 * HD), bf16),
            pltpu.VMEM((LAYERS, SOURCES, HEADS * ROWS, 2 * HD), bf16),
            pltpu.VMEM((LAYERS, SOURCES, CORES * CHIPS * ROWS, 2 * HD), bf16),
            pltpu.VMEM((far, HEADS * TOK, 2 * HD), bf16),
            pltpu.VMEM((POOL, HEADS * TOK, 2 * HD), bf16),
            pltpu.VMEM((ENTRIES, HEADS * TOK, 2 * HD), bf16),
            pltpu.VMEM((LAYERS, SPAN, QH * HD), bf16),
            pltpu.VMEM((LAYERS, QH, 1, SPAN), jnp.float32),
            pltpu.VMEM((LAYERS, QH, 1, SPAN), jnp.float32),
            pltpu.VMEM((LAYERS, QH, HD, SPAN), jnp.float32),
            pltpu.VMEM((LAYERS, QH, HD, SPAN), bf16),
            pltpu.VMEM((HD, max(high - low for low, high in GROUPS) * KEYS), bf16),
            pltpu.VMEM((KEYS, SPAN), jnp.float32),
            pltpu.SemaphoreType.DMA((6,)),
            pltpu.SemaphoreType.DMA((LAYERS,)),
            pltpu.SemaphoreType.DMA((LAYERS, far)),
            pltpu.SemaphoreType.DMA((LAYERS, N_GROUPS)),
            pltpu.SemaphoreType.DMA((LAYERS, N_GROUPS)),
            pltpu.SemaphoreType.DMA((LAYERS, N_GROUPS)),
            pltpu.SemaphoreType.DMA((LAYERS, N_GROUPS)),
            pltpu.SemaphoreType.DMA((1,)),
            pltpu.SemaphoreType.DMA((1,)),
            pltpu.SemaphoreType.DMA((LAYERS + 1,)),
        ],
        compiler_params=pltpu.CompilerParams(
            collective_id=0, has_side_effects=True, vmem_limit_bytes=60 << 20
        ),
    )(
        block_ids[0],
        prefix_count,
        new_ids[0].transpose(1, 2, 0),
        queries[0, 0],
        pool_cache.reshape(SLOTS, HEADS * TOK, 2 * HD),
        new_kv.reshape(ENTRIES, HEADS * TOK, 2 * HD),
    )
    return attn[None, None], stored.reshape(1, ENTRIES, HEADS, TOK, 2 * HD)


def solution(mesh):
    in_specs = (
        P("rep", "pool", None, None, "tp"),
        P("pool", None, "tp", None),
        P("rep", "pool", None, None, None, "tp", None),
        P("rep", None, None, None),
        P("rep", None),
        P("rep", None, None, None),
    )
    out_specs = (P("rep", "pool", None, None, "tp"), P("rep", "pool", None, "tp", None))
    return jax.shard_map(body, mesh=mesh, in_specs=in_specs, out_specs=out_specs, check_vma=False)
```
